256 devices in a mesh: pool: 32 (over z, y_hi, core), tensor: 8 (over y_lo, x).
Axes of the slice: x: 4, y: 4 (y_hi: 2, y_lo: 2; y = y_hi * 2 + y_lo), z: 8, core: 2. Of those that a mesh axis runs over, the one named last changes fastest.
Arguments:
- queries: bfloat16 [8192, 8192], P(('pool', 'tensor')), may hold values from -4.5 to 4.5
- new_keys: bfloat16 [8192, 1024], P(('pool', 'tensor')), may hold values from -4.5 to 4.5
- new_values: bfloat16 [8192, 1024], P(('pool', 'tensor')), may hold values from -40 to 40
- pool_keys: bfloat16 [8192, 16, 1024], P('pool', None, 'tensor'), may hold values from -4.5 to 4.5
- pool_values: bfloat16 [8192, 16, 1024], P('pool', None, 'tensor'), may hold values from -40 to 40
- prefix_blocks: int32 [32, 256], replicated, may hold values from 0 to 8191, as said below
- block_owner: int32 [8192], replicated, may hold values from 0 to 31, as said below
- block_slot: int32 [8192], replicated, may hold values from 0 to 255
- evict_slots: int32 [32, 16], replicated, may hold values from 0 to 8191, as said below
- tok_counts: int32 [32], replicated, may hold values from 1 to 256, 5120 in all
Outputs:
- attended: bfloat16 [8192, 8192], P(('pool', 'tensor'))
- new_pool_keys: bfloat16 [8192, 16, 1024], P('pool', None, 'tensor')
- new_pool_values: bfloat16 [8192, 16, 1024], P('pool', None, 'tensor')
The draws below stay inside these ranges and needn't reach their ends.
Inputs may be any that keep to these rules, and one draw needn't show every extreme that they name: `block_owner`: together with block_slot it puts every block in its own slot. `prefix_blocks`: A group's 256 ids are distinct; at most 12 of them are held by one owner, and in each group some owner holds exactly 12. Groups share blocks. `evict_slots`: all entries are distinct; at most 1 of a group's blocks go to one owner (slot // 256), and one owner receives exactly 1 from every group. `tok_counts`: one group has 256 live tokens.
All inputs are finite; a program needn't handle non-finite values.
Results may differ from the reference program's by a relative error of at most 0.0065.
Values may be sent and summed in bfloat16 or wider, within the bound.
No kernel may reach another device: no remote copies, remote signals or barrier semaphores. Data moves between devices by JAX's collectives and lax.ppermute only.
A program may use at most 64 MiB of HBM per device.

```python
import math
import jax
import jax.numpy as jnp
import numpy as np
from jax import lax

H = 64
KVH = 8
HD = 128
TOK_DEV = 256
PBLK = 256
BLK = 16
GROUPS = 32
TOKENS = 8192
SLOTS = 256
NBLK = 8192
CAP = 12
NEWB = 16
WCAP = 1


def pool_places(key):
    return jax.random.permutation(jax.random.fold_in(key, 101), NBLK).astype(jnp.int32)


def draw_queries(key, part):
    key = jax.random.fold_in(key, 11)
    first = jax.random.fold_in(key, 0)
    base = jax.random.normal(first, (TOKENS, H * HD), jnp.float32)
    return jnp.clip(base, -4.5, 4.5).astype(jnp.bfloat16)


def draw_pool_keys(key, part):
    key = jax.random.fold_in(key, 13)
    first = jax.random.fold_in(key, 0)
    rows = NBLK * BLK
    base = 1.2 * jax.random.normal(first, (rows, KVH * HD), jnp.float32)
    return jnp.clip(base, -4.5, 4.5).reshape(NBLK, BLK, KVH * HD).astype(jnp.bfloat16)


def draw_block_owner(key, part):
    places = pool_places(key)
    return (places // SLOTS).astype(jnp.int32)


def draw_block_slot(key, part):
    places = pool_places(key)
    return (places % SLOTS).astype(jnp.int32)


def draw_prefix_blocks(key, part):
    places = pool_places(key)
    key = jax.random.fold_in(key, 23)
    inverse = jnp.zeros((NBLK,), jnp.int32).at[places].set(jnp.arange(NBLK, dtype=jnp.int32))
    candidates = jnp.arange(GROUPS * CAP, dtype=jnp.int32)

    def one_group(index):
        group_key = jax.random.fold_in(key, index)
        order_key, forced_key, offset_key = jax.random.split(group_key, 3)
        order_score = jax.random.permutation(order_key, GROUPS * CAP).astype(jnp.int32)
        forced = jax.random.randint(forced_key, (), 0, GROUPS, jnp.int32)
        score = jnp.where(candidates // CAP == forced, order_score - GROUPS * CAP, order_score)
        chosen = jnp.argsort(score, stable=True)[:PBLK].astype(jnp.int32)
        owner = chosen // CAP
        rank = chosen % CAP
        offset = jax.random.randint(offset_key, (GROUPS,), 0, 4, jnp.int32)
        slot = (offset[owner] + rank) % SLOTS
        return inverse[owner * SLOTS + slot]
    return jax.vmap(one_group)(jnp.arange(GROUPS, dtype=jnp.int32))


def draw_evict_slots(key, part):
    key = jax.random.fold_in(key, 29)
    forced_key, perm_key, order_key = jax.random.split(key, 3)
    forced = jax.random.randint(forced_key, (), 0, GROUPS, jnp.int32)
    owner_perms = jax.vmap(lambda owner: jax.random.permutation(jax.random.fold_in(perm_key, owner), SLOTS).astype(jnp.int32))(jnp.arange(GROUPS, dtype=jnp.int32))
    candidates = jnp.arange(GROUPS * WCAP, dtype=jnp.int32)

    def one_group(index):
        order_score = jax.random.permutation(jax.random.fold_in(order_key, index), GROUPS * WCAP).astype(jnp.int32)
        score = jnp.where(candidates // WCAP == forced, order_score - GROUPS * WCAP, order_score)
        chosen = jnp.argsort(score, stable=True)[:NEWB].astype(jnp.int32)
        owner = chosen // WCAP
        rank = chosen % WCAP
        slot = owner_perms[owner, index * WCAP + rank]
        return (owner * SLOTS + slot).astype(jnp.int32)
    return jax.vmap(one_group)(jnp.arange(GROUPS, dtype=jnp.int32))


def steps_of(key, shape, cuts, least, top_value):
    gain, own = 1.0, jax.random.fold_in(key, 6)
    for dim, parts in cuts:
        heights = jnp.exp(jax.random.uniform(jax.random.fold_in(own, dim), (parts,), jnp.float32, least / len(cuts), top_value / len(cuts)))
        gain = gain * jnp.repeat(heights, shape[dim] // parts).reshape([-1 if axis == dim else 1 for axis in range(len(shape))])
    return gain


def split_up(amount, total, limit, slope):
    loads = [(1 << 20) // math.isqrt(grade ** slope) + 1 for grade in range(2, amount + 1)]
    rest, given = total - limit - (amount - 1), [1] * (amount - 1)
    while rest > 0:
        free = [i for i in range(amount - 1) if given[i] < limit]
        mass, budget = sum([loads[i] for i in free]), rest
        for i in free:
            extra = min(limit - given[i], max(1, budget * loads[i] // mass), rest)
            given[i] = given[i] + extra
            rest = rest - extra
    return np.array([limit] + given)


def uneven_parts(stream_key, number_of, total, bound, lean):
    if number_of == 2:
        one = jax.random.randint(stream_key, (), max(1, total - bound), min(bound, total - 1) + 1)
        return jnp.stack([one, total - one])
    tallies = jnp.asarray(split_up(number_of, total, bound, lean), jnp.int32)
    twos = (number_of - 1) // 2
    source_of, receiver = tallies[1:1 + 2 * twos:2], tallies[2:2 + 2 * twos:2]
    margin = jnp.minimum(source_of - 1, bound - receiver)
    shifted = jax.random.randint(jax.random.fold_in(stream_key, 1), (twos,), 0, 1 << 20) % (margin + 1)
    tallies = tallies.at[1:1 + 2 * twos:2].set(source_of - shifted).at[2:2 + 2 * twos:2].set(receiver + shifted)
    return tallies[jax.random.permutation(jax.random.fold_in(stream_key, 2), number_of)]


def normal_values(key, shape, scale, most, cuts=(), kind=jnp.bfloat16):
    loudness = steps_of(key, shape, cuts, -0.22, 0.18) if cuts else 1.0
    values = jax.random.normal(key, shape, jnp.float32) * scale * loudness
    return jnp.minimum(jnp.maximum(values, -most), most).astype(kind)


def setup_inputs(seed: int = 0) -> dict:
    arg_keys = jax.random.split(jax.random.key(seed), 11)
    queries = draw_queries(jax.random.fold_in(arg_keys[10], 71), 0)
    new_keys = normal_values(arg_keys[1], (TOKENS, KVH * HD), 1.8, 4.5, ((0, 256),))
    new_values = normal_values(arg_keys[2], (TOKENS, KVH * HD), 8.0, 40.0, ((0, 256),))
    pool_keys = draw_pool_keys(jax.random.fold_in(arg_keys[10], 71), 0)
    pool_values = normal_values(arg_keys[4], (NBLK, BLK, KVH * HD), 8.0, 40.0, ((0, 32), (2, 8)))
    prefix_blocks = draw_prefix_blocks(jax.random.fold_in(arg_keys[10], 71), 0)
    block_owner = draw_block_owner(jax.random.fold_in(arg_keys[10], 71), 0)
    block_slot = draw_block_slot(jax.random.fold_in(arg_keys[10], 71), 0)
    evict_slots = draw_evict_slots(jax.random.fold_in(arg_keys[10], 71), 0)
    tok_counts = uneven_parts(arg_keys[9], GROUPS, GROUPS * TOK_DEV * 5 // 8, TOK_DEV, 2).astype(jnp.int32)
    return dict(queries=queries, new_keys=new_keys, new_values=new_values, pool_keys=pool_keys, pool_values=pool_values, prefix_blocks=prefix_blocks, block_owner=block_owner, block_slot=block_slot, evict_slots=evict_slots, tok_counts=tok_counts)


neg_big = -1.0e30


def group_output(query_rows, prefix_keys, prefix_values, own_keys, own_values, count):
    tok = query_rows.shape[0]
    group = H // KVH
    span = prefix_keys.shape[0]
    queries_f = jnp.moveaxis(query_rows.astype(jnp.float32).reshape(tok, KVH, group, HD), 1, 0)
    keys_pre = jnp.moveaxis(prefix_keys.astype(jnp.float32).reshape(span, KVH, HD), 1, 0)
    values_pre = jnp.moveaxis(prefix_values.astype(jnp.float32).reshape(span, KVH, HD), 1, 0)
    keys_own = jnp.moveaxis(own_keys.astype(jnp.float32).reshape(tok, KVH, HD), 1, 0)
    values_own = jnp.moveaxis(own_values.astype(jnp.float32).reshape(tok, KVH, HD), 1, 0)
    position = jnp.arange(tok, dtype=jnp.int32)
    causal = position[None, :] <= position[:, None]
    scale = HD ** -0.5
    highest = lax.Precision.HIGHEST

    def per_head(pieces):
        q_head, k_pre, v_pre, k_own, v_own = pieces
        s_pre = jnp.einsum("tgd,sd->gts", q_head, k_pre, precision=highest) * scale
        s_own = jnp.einsum("tgd,sd->gts", q_head, k_own, precision=highest) * scale
        s_own = jnp.where(causal, s_own, neg_big)
        best = jnp.maximum(jnp.max(s_pre, axis=2), jnp.max(s_own, axis=2))
        w_pre = jnp.exp(s_pre - best[..., None])
        w_own = jnp.where(causal, jnp.exp(s_own - best[..., None]), 0.0)
        total = jnp.sum(w_pre, axis=2) + jnp.sum(w_own, axis=2)
        r_pre = lax.optimization_barrier(w_pre.astype(jnp.bfloat16)).astype(jnp.float32)
        r_own = lax.optimization_barrier(w_own.astype(jnp.bfloat16)).astype(jnp.float32)
        summed = jnp.einsum("gts,sd->gtd", r_pre, v_pre, precision=highest)
        summed = summed + jnp.einsum("gts,sd->gtd", r_own, v_own, precision=highest)
        return summed / total[..., None]

    heads = lax.map(per_head, (queries_f, keys_pre, values_pre, keys_own, values_own))
    result = jnp.transpose(heads, (2, 0, 1, 3)).reshape(tok, H * HD)
    return jnp.where((position < count)[:, None], result, 0.0).astype(jnp.bfloat16)


def reference(queries, new_keys, new_values, pool_keys, pool_values, prefix_blocks, block_owner, block_slot, evict_slots, tok_counts):
    width = KVH * HD

    def one_group(index):
        start = (index * TOK_DEV).astype(jnp.int32)
        query_rows = lax.dynamic_slice_in_dim(queries, start, TOK_DEV, 0)
        own_keys = lax.dynamic_slice_in_dim(new_keys, start, TOK_DEV, 0)
        own_values = lax.dynamic_slice_in_dim(new_values, start, TOK_DEV, 0)
        block_ids = prefix_blocks[index]
        held = (block_owner[block_ids] * SLOTS + block_slot[block_ids]).astype(jnp.int32)
        prefix_keys = pool_keys[held].reshape(PBLK * BLK, width)
        prefix_values = pool_values[held].reshape(PBLK * BLK, width)
        return group_output(query_rows, prefix_keys, prefix_values, own_keys, own_values, tok_counts[index])

    attended = lax.map(one_group, jnp.arange(GROUPS, dtype=jnp.int32)).reshape(TOKENS, H * HD)
    row_index = jnp.arange(TOKENS, dtype=jnp.int32)
    keep = (row_index % TOK_DEV) < tok_counts[row_index // TOK_DEV]
    fresh_keys = jnp.where(keep[:, None], new_keys, jnp.zeros((), new_keys.dtype)).reshape(GROUPS * NEWB, BLK, width)
    fresh_values = jnp.where(keep[:, None], new_values, jnp.zeros((), new_values.dtype)).reshape(GROUPS * NEWB, BLK, width)
    target = evict_slots.reshape(-1).astype(jnp.int32)
    new_pool_keys = pool_keys.at[target].set(fresh_keys)
    new_pool_values = pool_values.at[target].set(fresh_values)
    return attended, new_pool_keys, new_pool_values
```

```python
import jax
import jax.numpy as jnp
from jax import lax
from jax.experimental import pallas as pl
from jax.experimental.pallas import tpu as pltpu
from jax.sharding import PartitionSpec as P

H = 64
KVH = 8
HD = 128
GROUP = H // KVH
BLK = 16
POOL = 32
PLANE = 4
LEVELS = 8
TENSOR = 8
SLOTS = 256
PBLK = 256
CAP = 12
TOK = 256
PIECE = (GROUP + 2) * HD
STEP = 4
SCALE = HD ** (-0.5) * 1.4426950408889634
neg_big = -1e30

bf16 = jnp.bfloat16
f32 = jnp.float32
i32 = jnp.int32

VMEM = pl.BlockSpec(memory_space=pltpu.VMEM)
SMEM = pl.BlockSpec(memory_space=pltpu.SMEM)


def cost(flops, moved, exps=0):
    return pl.CostEstimate(flops=flops, bytes_accessed=moved, transcendentals=exps)


def pack_kernel(me, prefix, owner, slot, keys, values, out, wanted, picked, picked_s, sem):
    step = pl.program_id(0)

    @pl.when(step == 0)
    def _():
        rows, lanes = owner.shape
        mine = jnp.where(owner[...] == me[0], slot[...] + 1, 0).astype(f32).astype(bf16)
        lane_of = lax.broadcasted_iota(i32, (lanes, PBLK), 0)
        row_of = lax.broadcasted_iota(i32, (rows, PBLK), 0)
        for g in range(POOL):
            index = prefix[g : g + 1, :]
            low = index & (lanes - 1)
            high = index >> 7
            hot = jnp.where(lane_of == low, 1.0, 0.0).astype(bf16)
            found = jnp.dot(mine, hot, preferred_element_type=f32)
            wanted[g : g + 1, :] = jnp.sum(
                jnp.where(row_of == high, found, 0.0), axis=0, keepdims=True
            )
        place = wanted[...]
        held = place > 0.5
        before = lax.broadcasted_iota(i32, (PBLK, PBLK), 0)
        after = lax.broadcasted_iota(i32, (PBLK, PBLK), 1)
        triangle = jnp.where(before <= after, 1.0, 0.0).astype(bf16)
        rank = jnp.dot(
            jnp.where(held, 1.0, 0.0).astype(bf16), triangle, preferred_element_type=f32
        )
        rank = jnp.where(held, rank, 0.0)
        lane = lax.broadcasted_iota(i32, (POOL, 128), 1)
        chosen = jnp.zeros((POOL, 128), f32)
        for r in range(CAP):
            one = jnp.sum(jnp.where(rank == r + 1.0, place - 1.0, 0.0), axis=1, keepdims=True)
            chosen = jnp.where(lane == r, one, chosen)
        picked[...] = chosen.astype(i32)
        copy = pltpu.make_async_copy(picked, picked_s, sem)
        copy.start()
        copy.wait()

    for g in range(POOL // STEP):
        for r in range(CAP):
            s = picked_s[step * (POOL // STEP) + g, r]
            out[g, r] = keys[s]
            out[g, CAP + r] = values[s]


def pack(me, prefix_blocks, block_owner, block_slot, pool_keys, pool_values):
    whole = lambda shape: pl.BlockSpec(shape, lambda i: (0,) * len(shape))
    table = (block_owner.shape[0] // 128, 128)
    return pl.pallas_call(
        pack_kernel,
        grid=(STEP,),
        out_shape=jax.ShapeDtypeStruct((POOL, 2 * CAP, BLK, HD), bf16),
        in_specs=[
            SMEM,
            whole(prefix_blocks.shape),
            whole(table),
            whole(table),
            whole(pool_keys.shape),
            whole(pool_values.shape),
        ],
        out_specs=pl.BlockSpec((POOL // STEP, 2 * CAP, BLK, HD), lambda i: (i, 0, 0, 0)),
        scratch_shapes=[
            pltpu.VMEM((POOL, PBLK), f32),
            pltpu.VMEM((POOL, 128), i32),
            pltpu.SMEM((POOL, 128), i32),
            pltpu.SemaphoreType.DMA,
        ],
        compiler_params=pltpu.CompilerParams(vmem_limit_bytes=24 * 1024 * 1024),
        cost_estimate=cost(10**9, 5 * 10**6),
        name="pack_blocks",
    )(
        me.reshape(1),
        prefix_blocks,
        block_owner.reshape(table),
        block_slot.reshape(table),
        pool_keys,
        pool_values,
    )


def gather_kernel(info, source, *refs):
    pieces = refs[:TENSOR]
    heads, own_keys, own_values = refs[TENSOR : TENSOR + 3]
    sends = refs[TENSOR + 3 : TENSOR + 3 + LEVELS]
    fresh = refs[-1]
    t, count, level = info[0], info[1], info[2]
    rows = TOK // TENSOR
    for k in range(TENSOR):
        start = pl.multiple_of((t ^ k) * rows, rows)
        at = pl.ds(start, rows)
        for h in range(GROUP):
            heads[h, at, :] = pieces[k][:, h * HD : (h + 1) * HD]
        key_rows = pieces[k][:, GROUP * HD : (GROUP + 1) * HD]
        value_rows = pieces[k][:, (GROUP + 1) * HD :]
        own_keys[at, :] = key_rows
        own_values[at, :] = value_rows
        live = start + lax.broadcasted_iota(i32, (rows, HD), 0) < count
        kept_keys = jnp.where(live, key_rows.astype(f32), 0.0).astype(bf16)
        kept_values = jnp.where(live, value_rows.astype(f32), 0.0).astype(bf16)
        for b in range(rows // BLK):
            block = (t ^ k) * (rows // BLK) + b
            fresh[block, 0] = kept_keys[b * BLK : (b + 1) * BLK]
            fresh[block, 1] = kept_values[b * BLK : (b + 1) * BLK]
    for k in range(LEVELS):
        plane = lax.rem(level + k, LEVELS)
        for r in range(PLANE):
            sends[k][r] = fresh[source[plane * PLANE + r]]


def gather(info, source, pieces):
    return pl.pallas_call(
        gather_kernel,
        out_shape=[
            jax.ShapeDtypeStruct((GROUP, TOK, HD), bf16),
            jax.ShapeDtypeStruct((TOK, HD), bf16),
            jax.ShapeDtypeStruct((TOK, HD), bf16),
        ]
        + [jax.ShapeDtypeStruct((PLANE, 2, BLK, HD), bf16)] * LEVELS,
        in_specs=[SMEM, SMEM] + [VMEM] * TENSOR,
        out_specs=[VMEM] * (3 + LEVELS),
        scratch_shapes=[pltpu.VMEM((TOK // BLK, 2, BLK, HD), bf16)],
        compiler_params=pltpu.CompilerParams(vmem_limit_bytes=16 * 1024 * 1024),
        cost_estimate=cost(10**6, 2 * 10**6),
        name="gather_rows",
    )(info, source, *pieces)


def turn_kernel(info, *refs):
    got = refs[:LEVELS]
    outs = refs[LEVELS:]
    lane = info[3]
    for m in range(PLANE):
        for k in range(LEVELS):
            outs[m][k] = got[k][lane ^ m]


def turn(info, got):
    return pl.pallas_call(
        turn_kernel,
        out_shape=[jax.ShapeDtypeStruct((LEVELS, 2, BLK, HD), bf16)] * PLANE,
        in_specs=[SMEM] + [VMEM] * LEVELS,
        out_specs=[VMEM] * PLANE,
        cost_estimate=cost(10**6, 10**6),
        name="turn_blocks",
    )(info, *got)


def write_kernel(info, target, keys, values, *refs):
    arrived = refs[:PLANE]
    out_keys, out_values = refs[PLANE:]
    level, lane = info[2], info[3]
    out_keys[...] = keys[...]
    out_values[...] = values[...]
    for m in range(PLANE):
        for k in range(LEVELS):
            group = lax.rem(level + LEVELS - k, LEVELS) * PLANE + (lane ^ m)
            slot = target[group]

            @pl.when(slot >= 0)
            def _():
                out_keys[slot] = arrived[m][k, 0]
                out_values[slot] = arrived[m][k, 1]


def write(info, target, pool_keys, pool_values, arrived):
    return pl.pallas_call(
        write_kernel,
        out_shape=[jax.ShapeDtypeStruct(pool_keys.shape, bf16)] * 2,
        in_specs=[SMEM, SMEM] + [VMEM] * (2 + PLANE),
        out_specs=[VMEM] * 2,
        compiler_params=pltpu.CompilerParams(vmem_limit_bytes=16 * 1024 * 1024),
        cost_estimate=cost(10**6, 4 * 10**6),
        name="write_blocks",
    )(info, target, pool_keys, pool_values, *arrived)


KEYS = PBLK * BLK
TILE = 512
TILES = KEYS // TILE
ALL = KEYS + TOK


def attend_kernel(
    info, where_from, heads, next_heads, own_keys, own_values, got, out, keys, values, scores, peak
):
    step = pl.program_id(0)
    slot = lax.rem(step, 2)
    nt = (((1,), (1,)), ((), ()))

    def first_pass(query, into):
        best = None
        for j in range(TILES):
            part = lax.dot_general(
                query, keys[j * TILE : (j + 1) * TILE, :], nt, preferred_element_type=f32
            )
            scores[into, :, j * TILE : (j + 1) * TILE] = part
            for c in range(TILE // 128):
                piece = part[:, c * 128 : (c + 1) * 128]
                best = piece if best is None else jnp.maximum(best, piece)
        part = lax.dot_general(query, own_keys[...], nt, preferred_element_type=f32)
        row = lax.broadcasted_iota(i32, (TOK, TOK), 0)
        column = lax.broadcasted_iota(i32, (TOK, TOK), 1)
        part = jnp.where(column <= row, part, neg_big)
        scores[into, :, KEYS:] = part
        for c in range(TOK // 128):
            best = jnp.maximum(best, part[:, c * 128 : (c + 1) * 128])
        top = jnp.max(best, axis=1, keepdims=True)
        peak[into] = jnp.broadcast_to(top * SCALE, (TOK, 128))

    @pl.when(step == 0)
    def _():
        for b in range(PBLK):
            index = where_from[b]
            keys[b * BLK : (b + 1) * BLK, :] = got[index]
            values[b * BLK : (b + 1) * BLK, :HD] = got[index + CAP]
        values[KEYS:, :HD] = own_values[...]
        values[:, HD:] = jnp.ones((ALL, HD), bf16)
        first_pass(heads[0], 0)

    first_pass(next_heads[0], 1 - slot)
    top = peak[slot]
    summed = jnp.zeros((TOK, 2 * HD), f32)
    for begin, width in [(j * TILE, TILE) for j in range(TILES)] + [(KEYS, TOK)]:
        part = scores[slot, :, begin : begin + width]
        weights = jnp.concatenate(
            [
                jnp.exp2(part[:, c * 128 : (c + 1) * 128] * SCALE - top)
                for c in range(width // 128)
            ],
            axis=1,
        ).astype(bf16)
        summed += jnp.dot(weights, values[begin : begin + width, :], preferred_element_type=f32)
    live = lax.broadcasted_iota(i32, (TOK, HD), 0) < info[1]
    result = summed[:, :HD] / summed[:, HD:]
    out[...] = jnp.where(live, result, 0.0).astype(bf16)


def attend(info, where_from, heads, own_keys, own_values, got):
    whole = lambda shape: pl.BlockSpec(shape, lambda i: (0,) * len(shape))
    blocks = got.shape[0] * got.shape[1]
    return pl.pallas_call(
        attend_kernel,
        grid=(GROUP,),
        out_shape=jax.ShapeDtypeStruct((TOK, GROUP * HD), bf16),
        in_specs=[
            SMEM,
            SMEM,
            pl.BlockSpec((1, TOK, HD), lambda i: (i, 0, 0)),
            pl.BlockSpec((1, TOK, HD), lambda i: (jnp.minimum(i + 1, GROUP - 1), 0, 0)),
            whole((TOK, HD)),
            whole((TOK, HD)),
            whole((blocks, BLK, HD)),
        ],
        out_specs=pl.BlockSpec((TOK, HD), lambda i: (0, i)),
        scratch_shapes=[
            pltpu.VMEM((KEYS, HD), bf16),
            pltpu.VMEM((ALL, 2 * HD), bf16),
            pltpu.VMEM((2, TOK, ALL), f32),
            pltpu.VMEM((2, TOK, 128), f32),
        ],
        compiler_params=pltpu.CompilerParams(vmem_limit_bytes=48 * 1024 * 1024),
        cost_estimate=cost(9 * 10**9, 6 * 10**6, 9 * 10**6),
        name="attend",
    )(info, where_from, heads, heads, own_keys, own_values, got.reshape(blocks, BLK, HD))


def local(
    queries,
    new_keys,
    new_values,
    pool_keys,
    pool_values,
    prefix_blocks,
    block_owner,
    block_slot,
    evict_slots,
    tok_counts,
):
    me = lax.axis_index("pool").astype(i32)
    t = lax.axis_index("tensor").astype(i32)

    send = pack(me, prefix_blocks, block_owner, block_slot, pool_keys, pool_values)
    send, queries, new_keys, new_values = lax.optimization_barrier(
        (send, queries, new_keys, new_values)
    )
    got = lax.all_to_all(send, "pool", split_axis=0, concat_axis=0, tiled=True)

    pieces = []
    for k in range(TENSOR):
        head = t ^ k
        piece = jnp.concatenate(
            [
                lax.dynamic_slice_in_dim(queries, head * GROUP * HD, GROUP * HD, 1),
                lax.dynamic_slice_in_dim(new_keys, head * HD, HD, 1),
                lax.dynamic_slice_in_dim(new_values, head * HD, HD, 1),
            ],
            axis=1,
        )
        if k:
            piece = lax.ppermute(piece, "tensor", [(s, s ^ k) for s in range(TENSOR)])
        pieces.append(piece)

    sources = jnp.arange(POOL, dtype=i32)
    my_owners = block_owner[prefix_blocks[me]]
    ends = jnp.sum((my_owners[None, :] <= sources[:, None]).astype(i32), axis=1)
    starts = jnp.sum((my_owners[None, :] < sources[:, None]).astype(i32), axis=1)
    nth = jnp.arange(PBLK, dtype=i32)
    which = jnp.sum((ends[None, :] <= nth[:, None]).astype(i32), axis=1)
    base = jnp.max(jnp.where(starts[None, :] <= nth[:, None], starts[None, :], 0), axis=1)
    where_from = which * (2 * CAP) + nth - base

    targets = evict_slots // SLOTS
    places = evict_slots % SLOTS
    order = jnp.arange(evict_slots.shape[1], dtype=i32)
    source = jnp.sum(
        jnp.where(targets[me][None, :] == sources[:, None], order[None, :], 0), axis=1
    )
    target = jnp.max(jnp.where(targets == me, places, -1), axis=1)

    info = jnp.stack([t, tok_counts[me], me // PLANE, me % PLANE])
    heads, own_keys, own_values, *sends = gather(info, source, pieces)
    arrived = [sends[0]] + [
        lax.ppermute(
            sends[k], "pool", [(s, (s + PLANE * k) % POOL) for s in range(POOL)]
        )
        for k in range(1, LEVELS)
    ]
    turned = turn(info, arrived)
    arrived = [turned[0]] + [
        lax.ppermute(turned[m], "pool", [(s, s ^ m) for s in range(POOL)])
        for m in range(1, PLANE)
    ]
    new_pool_keys, new_pool_values = write(info, target, pool_keys, pool_values, arrived)

    result = attend(info, where_from, heads, own_keys, own_values, got)
    result = result.reshape(TENSOR, TOK // TENSOR, GROUP * HD)
    attended = lax.all_to_all(result, "tensor", split_axis=0, concat_axis=0, tiled=True)
    attended = jnp.transpose(attended, (1, 0, 2)).reshape(TOK // TENSOR, H * HD)
    return (attended, new_pool_keys, new_pool_values)


def solution(mesh):
    placed = (
        P(("pool", "tensor"), None),
        P(("pool", "tensor"), None),
        P(("pool", "tensor"), None),
        P("pool", None, "tensor"),
        P("pool", None, "tensor"),
        P(),
        P(),
        P(),
        P(),
        P(),
    )
    return jax.shard_map(
        local,
        mesh=mesh,
        in_specs=placed,
        out_specs=(
            P(("pool", "tensor"), None),
            P("pool", None, "tensor"),
            P("pool", None, "tensor"),
        ),
        check_vma=False,
    )
```

```python
import jax
import jax.numpy as jnp
from jax import lax
from jax.experimental import pallas as pl
from jax.experimental.pallas import tpu as pltpu
from jax.sharding import PartitionSpec as P

H = 64
KVH = 8
HD = 128
GROUP = H // KVH
BLK = 16
POOL = 32
TENSOR = 8
SLOTS = 256
PBLK = 256
CAP = 12
TOK = 256
NEWB = TOK // BLK
LOAD = 2 * CAP
PART = 8
WIDE = 60 * 1024 * 1024
SCALE = HD ** (-0.5) * 1.4426950408889634
neg_big = -1e30

bf16 = jnp.bfloat16
f32 = jnp.float32
i32 = jnp.int32

VMEM = pl.BlockSpec(memory_space=pltpu.VMEM)
SMEM = pl.BlockSpec(memory_space=pltpu.SMEM)
HBM = pl.BlockSpec(memory_space=pltpu.HBM)
NT = (((1,), (1,)), ((), ()))


def cost(flops, moved, exps=0):
    return pl.CostEstimate(flops=flops, bytes_accessed=moved, transcendentals=exps)


def pack_kernel(me, prefix_h, owner_h, slot_h, keys_h, values_h, out_h, *scratch):
    prefix, owner, slot, keys, values, wanted, picked, picked_s, out, sems, out_sems = scratch
    sources = (prefix_h, owner_h, slot_h, keys_h, values_h)
    copies = [
        pltpu.make_async_copy(source, target, sems.at[i])
        for i, (source, target) in enumerate(zip(sources, scratch[:5]))
    ]
    for copy in copies:
        copy.start()
    for copy in copies[:3]:
        copy.wait()
    rows, lanes = owner.shape
    mine = jnp.where(owner[...] == me[0], slot[...] + 1, 0).astype(f32).astype(bf16)
    lane_of = lax.broadcasted_iota(i32, (lanes, PBLK), 0)
    row_of = lax.broadcasted_iota(i32, (rows, PBLK), 0)
    for g in range(POOL):
        index = prefix[g : g + 1, :]
        low = index & (lanes - 1)
        high = index >> 7
        hot = jnp.where(lane_of == low, 1.0, 0.0).astype(bf16)
        found = jnp.dot(mine, hot, preferred_element_type=f32)
        wanted[g : g + 1, :] = jnp.sum(
            jnp.where(row_of == high, found, 0.0), axis=0, keepdims=True
        )
    place = wanted[...]
    held = place > 0.5
    before = lax.broadcasted_iota(i32, (PBLK, PBLK), 0)
    after = lax.broadcasted_iota(i32, (PBLK, PBLK), 1)
    triangle = jnp.where(before <= after, 1.0, 0.0).astype(bf16)
    rank = jnp.dot(
        jnp.where(held, 1.0, 0.0).astype(bf16), triangle, preferred_element_type=f32
    )
    rank = jnp.where(held, rank, 0.0)
    lane = lax.broadcasted_iota(i32, (POOL, 128), 1)
    chosen = jnp.zeros((POOL, 128), f32)
    for r in range(CAP):
        one = jnp.sum(jnp.where(rank == r + 1.0, place - 1.0, 0.0), axis=1, keepdims=True)
        chosen = jnp.where(lane == r, one, chosen)
    picked[...] = chosen.astype(i32)
    listed = pltpu.make_async_copy(picked, picked_s, sems.at[5])
    listed.start()
    listed.wait()
    for copy in copies[3:]:
        copy.wait()

    leaving = []
    for part in range(POOL // PART):
        groups = pl.ds(part * PART, PART)

        @pl.loop(part * PART, (part + 1) * PART)
        def _(g):
            for r in range(CAP):
                s = picked_s[g, r]
                out[g, r] = keys[s]
                out[g, CAP + r] = values[s]

        leaving.append(
            pltpu.make_async_copy(out.at[groups], out_h.at[groups], out_sems.at[part])
        )
        leaving[-1].start()
    for copy in leaving:
        copy.wait()


def pack(me, prefix_blocks, block_owner, block_slot, pool_keys, pool_values):
    table = (block_owner.shape[0] // 128, 128)
    return pl.pallas_call(
        pack_kernel,
        out_shape=jax.ShapeDtypeStruct((POOL, LOAD, BLK, HD), bf16),
        in_specs=[SMEM] + [HBM] * 5,
        out_specs=HBM,
        scratch_shapes=[
            pltpu.VMEM(prefix_blocks.shape, i32),
            pltpu.VMEM(table, i32),
            pltpu.VMEM(table, i32),
            pltpu.VMEM(pool_keys.shape, bf16),
            pltpu.VMEM(pool_values.shape, bf16),
            pltpu.VMEM((POOL, PBLK), f32),
            pltpu.VMEM((POOL, 128), i32),
            pltpu.SMEM((POOL, 128), i32),
            pltpu.VMEM((POOL, LOAD, BLK, HD), bf16),
            pltpu.SemaphoreType.DMA((6,)),
            pltpu.SemaphoreType.DMA((POOL // PART,)),
        ],
        compiler_params=pltpu.CompilerParams(vmem_limit_bytes=WIDE),
        cost_estimate=cost(10**9, 5 * 10**6),
        name="pack_blocks",
    )(
        me.reshape(1),
        prefix_blocks,
        block_owner.reshape(table),
        block_slot.reshape(table),
        pool_keys,
        pool_values,
    )


def gather_kernel(info, evict, *refs):
    pieces = refs[:TENSOR]
    heads, shift, start, sends, own_keys, own_values = refs[TENSOR:]
    t, count, me = info[0], info[1], info[2]
    rows = TOK // TENSOR
    for k in range(TENSOR):
        begin = pl.multiple_of((t ^ k) * rows, rows)
        at = pl.ds(begin, rows)
        for h in range(GROUP):
            heads[pl.ds(pl.multiple_of(h * TOK + begin, rows), rows), :] = pieces[k][
                :, h * HD : (h + 1) * HD
            ]
        own_keys[at, :] = pieces[k][:, GROUP * HD : (GROUP + 1) * HD]
        own_values[at, :] = pieces[k][:, (GROUP + 1) * HD :]
    place = lax.broadcasted_iota(i32, (BLK, HD), 0)
    for j in range(NEWB):
        owner = evict[me, j] >> 8
        live = j * BLK + place < count
        for part, own in enumerate((own_keys, own_values)):
            block = own[j * BLK : (j + 1) * BLK, :]
            sends[owner, part] = jnp.where(live, block.astype(f32), 0.0).astype(bf16)
    both = jnp.concatenate([own_values[...], jnp.ones((TOK, HD), bf16)], axis=1)
    row = lax.broadcasted_iota(i32, (TOK, TOK), 0)
    column = lax.broadcasted_iota(i32, (TOK, TOK), 1)

    @pl.loop(0, GROUP)
    def _(h):
        at = pl.ds(pl.multiple_of(h * TOK, TOK), TOK)
        scores = lax.dot_general(heads[at, :], own_keys[...], NT, preferred_element_type=f32)
        scores = jnp.where(column <= row, scores * SCALE, neg_big)
        top = jnp.max(scores, axis=1, keepdims=True)
        shift[at, :] = jnp.broadcast_to(top, (TOK, HD))
        weights = jnp.exp2(scores - top).astype(bf16)
        start[at, :] = jnp.dot(weights, both, preferred_element_type=f32)


def gather(info, evict_slots, pieces):
    return pl.pallas_call(
        gather_kernel,
        out_shape=[
            jax.ShapeDtypeStruct((GROUP * TOK, HD), bf16),
            jax.ShapeDtypeStruct((GROUP * TOK, HD), f32),
            jax.ShapeDtypeStruct((GROUP * TOK, 2 * HD), f32),
            jax.ShapeDtypeStruct((POOL, 2, BLK, HD), bf16),
        ],
        in_specs=[SMEM, SMEM] + [VMEM] * TENSOR,
        out_specs=[VMEM] * 4,
        scratch_shapes=[pltpu.VMEM((TOK, HD), bf16), pltpu.VMEM((TOK, HD), bf16)],
        compiler_params=pltpu.CompilerParams(vmem_limit_bytes=16 * 1024 * 1024),
        cost_estimate=cost(10**9, 4 * 10**6),
        name="gather_rows",
    )(info, evict_slots, *pieces)


def write_kernel(target, keys, values, arrived, out_keys, out_values):
    out_keys[...] = keys[...]
    out_values[...] = values[...]
    for g in range(POOL):
        slot = target[g]

        @pl.when(slot >= 0)
        def _():
            out_keys[slot] = arrived[g, 0]
            out_values[slot] = arrived[g, 1]


def write(target, pool_keys, pool_values, arrived):
    return pl.pallas_call(
        write_kernel,
        out_shape=[jax.ShapeDtypeStruct(pool_keys.shape, bf16)] * 2,
        in_specs=[SMEM] + [VMEM] * 3,
        out_specs=[VMEM] * 2,
        compiler_params=pltpu.CompilerParams(vmem_limit_bytes=16 * 1024 * 1024),
        cost_estimate=cost(10**6, 4 * 10**6),
        name="write_blocks",
    )(target, pool_keys, pool_values, arrived)


KEYS = PBLK * BLK
ROWS = 1024
TILE = 256
SMALL = 256


def attend_kernel(
    info, where_from, heads_h, shift_h, start_h, got, out, keys, values, heads, shift, start, sems
):
    copies = [
        pltpu.make_async_copy(source, target, sems.at[i])
        for i, (source, target) in enumerate(
            [(heads_h, heads), (shift_h, shift), (start_h, start)]
        )
    ]
    for copy in copies:
        copy.start()
    for b in range(PBLK):
        index = where_from[b]
        keys[b * BLK : (b + 1) * BLK, :] = got[index]
        values[b * BLK : (b + 1) * BLK, :] = got[index + CAP]
    for copy in copies:
        copy.wait()
    ones = jnp.ones((TILE, HD), bf16)
    live = lax.broadcasted_iota(i32, (TOK, HD), 0) < info[1]

    def finish(h, summed):
        result = summed[:, :HD] / summed[:, HD:]
        out[:, h * HD : (h + 1) * HD] = jnp.where(live, result, 0.0).astype(bf16)

    for i in range(GROUP * TOK // ROWS):
        query = heads[i * ROWS : (i + 1) * ROWS, :]
        top = shift[i * ROWS : (i + 1) * ROWS, :]
        summed = start[i * ROWS : (i + 1) * ROWS, :]
        for j in range(KEYS // TILE):
            tile = slice(j * TILE, (j + 1) * TILE)
            part = lax.dot_general(query, keys[tile, :], NT, preferred_element_type=f32)
            weights = jnp.concatenate(
                [
                    jnp.exp2(part[:, c * HD : (c + 1) * HD] * SCALE - top)
                    for c in range(TILE // HD)
                ],
                axis=1,
            ).astype(bf16)
            both = jnp.concatenate([values[tile, :], ones], axis=1)
            summed = summed + jnp.dot(weights, both, preferred_element_type=f32)
        for h in range(ROWS // TOK):
            finish(i * (ROWS // TOK) + h, summed[h * TOK : (h + 1) * TOK, :])
        largest = jnp.max(summed[:, HD:])

        @pl.when(jnp.logical_not(largest < 1e30))
        def _():
            for h in range(ROWS // TOK):
                at = slice(i * ROWS + h * TOK, i * ROWS + (h + 1) * TOK)

                def one(j, state):
                    best, summed = state
                    tile = pl.ds(pl.multiple_of(j * SMALL, SMALL), SMALL)
                    part = (
                        lax.dot_general(
                            heads[at, :], keys[tile, :], NT, preferred_element_type=f32
                        )
                        * SCALE
                    )
                    above = jnp.maximum(best, jnp.max(part, axis=1, keepdims=True))
                    weights = jnp.exp2(part - above).astype(bf16)
                    both = jnp.concatenate([values[tile, :], ones], axis=1)
                    summed = summed * jnp.exp2(best - above) + jnp.dot(
                        weights, both, preferred_element_type=f32
                    )
                    return above, summed

                best, summed = lax.fori_loop(
                    0, KEYS // SMALL, one, (shift[at, :1], start[at, :])
                )
                finish(i * (ROWS // TOK) + h, summed)


def attend(info, where_from, heads, shift, start, got):
    blocks = got.shape[0] * got.shape[1]
    return pl.pallas_call(
        attend_kernel,
        out_shape=jax.ShapeDtypeStruct((TOK, GROUP * HD), bf16),
        in_specs=[SMEM, SMEM] + [HBM] * 3 + [VMEM],
        out_specs=VMEM,
        scratch_shapes=[
            pltpu.VMEM((KEYS, HD), bf16),
            pltpu.VMEM((KEYS, HD), bf16),
            pltpu.VMEM(heads.shape, bf16),
            pltpu.VMEM(shift.shape, f32),
            pltpu.VMEM(start.shape, f32),
            pltpu.SemaphoreType.DMA((3,)),
        ],
        compiler_params=pltpu.CompilerParams(vmem_limit_bytes=57 * 1024 * 1024),
        cost_estimate=cost(9 * 10**9, 6 * 10**6, 9 * 10**6),
        name="attend",
    )(info, where_from, heads, shift, start, got.reshape(blocks, BLK, HD))


def local(
    queries,
    new_keys,
    new_values,
    pool_keys,
    pool_values,
    prefix_blocks,
    block_owner,
    block_slot,
    evict_slots,
    tok_counts,
):
    me = lax.axis_index("pool").astype(i32)
    t = lax.axis_index("tensor").astype(i32)
    share = TOK // TENSOR
    info = jnp.stack([t, tok_counts[me], me])

    send = pack(me, prefix_blocks, block_owner, block_slot, pool_keys, pool_values)
    send, queries, new_keys, new_values = lax.optimization_barrier(
        (send, queries, new_keys, new_values)
    )
    got = lax.all_to_all(send, "pool", split_axis=0, concat_axis=0, tiled=True)

    pieces = []
    for k in range(TENSOR):
        head = t ^ k
        piece = jnp.concatenate(
            [
                lax.dynamic_slice_in_dim(queries, head * GROUP * HD, GROUP * HD, 1),
                lax.dynamic_slice_in_dim(new_keys, head * HD, HD, 1),
                lax.dynamic_slice_in_dim(new_values, head * HD, HD, 1),
            ],
            axis=1,
        )
        if k:
            piece = lax.ppermute(piece, "tensor", [(s, s ^ k) for s in range(TENSOR)])
        pieces.append(piece)

    sources = jnp.arange(POOL, dtype=i32)
    my_owners = block_owner[prefix_blocks[me]]
    ends = jnp.sum((my_owners[None, :] <= sources[:, None]).astype(i32), axis=1)
    starts = jnp.sum((my_owners[None, :] < sources[:, None]).astype(i32), axis=1)
    nth = jnp.arange(PBLK, dtype=i32)
    which = jnp.sum((ends[None, :] <= nth[:, None]).astype(i32), axis=1)
    base = jnp.max(jnp.where(starts[None, :] <= nth[:, None], starts[None, :], 0), axis=1)
    where_from = which * LOAD + nth - base

    target = jnp.max(jnp.where(evict_slots // SLOTS == me, evict_slots % SLOTS, -1), axis=1)

    heads, shift, start, sends = gather(info, evict_slots, pieces)
    got, sends = lax.optimization_barrier((got, sends))
    arrived = lax.all_to_all(sends, "pool", split_axis=0, concat_axis=0, tiled=True)
    result = attend(info, where_from, heads, shift, start, got)
    result, arrived = lax.optimization_barrier((result, arrived))
    result = result.reshape(TENSOR, share, GROUP * HD)
    attended = lax.all_to_all(result, "tensor", split_axis=0, concat_axis=0, tiled=True)
    attended = jnp.transpose(attended, (1, 0, 2)).reshape(share, H * HD)
    new_pool_keys, new_pool_values = write(target, pool_keys, pool_values, arrived)
    return (attended, new_pool_keys, new_pool_values)


def solution(mesh):
    placed = (
        P(("pool", "tensor"), None),
        P(("pool", "tensor"), None),
        P(("pool", "tensor"), None),
        P("pool", None, "tensor"),
        P("pool", None, "tensor"),
        P(),
        P(),
        P(),
        P(),
        P(),
    )
    return jax.shard_map(
        local,
        mesh=mesh,
        in_specs=placed,
        out_specs=(
            P(("pool", "tensor"), None),
            P("pool", None, "tensor"),
            P("pool", None, "tensor"),
        ),
        check_vma=False,
    )
```

```python
import jax
import jax.numpy as jnp
from jax import lax
from jax.experimental import pallas as pl
from jax.experimental.pallas import tpu as pltpu
from jax.sharding import PartitionSpec as P

H = 64
KVH = 8
HD = 128
GROUP = H // KVH
BLK = 16
POOL = 32
LANES = 4
LEVELS = POOL // LANES
TENSOR = 8
SLOTS = 256
PBLK = 256
CAP = 12
TOK = 256
NEWB = TOK // BLK
LOAD = 2 * CAP
PART = 8
WIDE = 57 * 1024 * 1024
SCALE = HD ** (-0.5) * 1.4426950408889634
neg_big = -1e30

bf16 = jnp.bfloat16
f32 = jnp.float32
i32 = jnp.int32

VMEM = pl.BlockSpec(memory_space=pltpu.VMEM)
SMEM = pl.BlockSpec(memory_space=pltpu.SMEM)
HBM = pl.BlockSpec(memory_space=pltpu.HBM)
NT = (((1,), (1,)), ((), ()))


def with_ones(values):
    return jnp.concatenate([values, jnp.ones(values.shape, bf16)], axis=1)


def cost(flops, moved, exps=0):
    return pl.CostEstimate(flops=flops, bytes_accessed=moved, transcendentals=exps)


def pack_kernel(me, prefix_h, owner_h, slot_h, keys_h, values_h, out_h, *scratch):
    prefix, owner, slot, keys, values, wanted, picked, picked_s, out, sems, out_sems = scratch
    sources = (prefix_h, owner_h, slot_h, keys_h, values_h)
    copies = [
        pltpu.make_async_copy(source, target, sems.at[i])
        for i, (source, target) in enumerate(zip(sources, scratch[:5]))
    ]
    for copy in copies:
        copy.start()
    for copy in copies[:3]:
        copy.wait()
    rows, lanes = owner.shape
    mine = jnp.where(owner[...] == me[0], slot[...] + 1, 0).astype(f32).astype(bf16)
    lane_of = lax.broadcasted_iota(i32, (lanes, PBLK), 0)
    row_of = lax.broadcasted_iota(i32, (rows, PBLK), 0)
    for g in range(POOL):
        index = prefix[g : g + 1, :]
        low = index & (lanes - 1)
        high = index >> 7
        hot = jnp.where(lane_of == low, 1.0, 0.0).astype(bf16)
        found = jnp.dot(mine, hot, preferred_element_type=f32)
        wanted[g : g + 1, :] = jnp.sum(
            jnp.where(row_of == high, found, 0.0), axis=0, keepdims=True
        )
    place = wanted[...]
    held = place > 0.5
    before = lax.broadcasted_iota(i32, (PBLK, PBLK), 0)
    after = lax.broadcasted_iota(i32, (PBLK, PBLK), 1)
    triangle = jnp.where(before <= after, 1.0, 0.0).astype(bf16)
    rank = jnp.dot(
        jnp.where(held, 1.0, 0.0).astype(bf16), triangle, preferred_element_type=f32
    )
    rank = jnp.where(held, rank, 0.0)
    lane = lax.broadcasted_iota(i32, (POOL, 128), 1)
    chosen = jnp.zeros((POOL, 128), f32)
    for r in range(CAP):
        one = jnp.sum(jnp.where(rank == r + 1.0, place - 1.0, 0.0), axis=1, keepdims=True)
        chosen = jnp.where(lane == r, one, chosen)
    picked[...] = chosen.astype(i32)
    listed = pltpu.make_async_copy(picked, picked_s, sems.at[5])
    listed.start()
    listed.wait()
    for copy in copies[3:]:
        copy.wait()

    leaving = []
    for part in range(POOL // PART):
        groups = pl.ds(part * PART, PART)

        @pl.loop(part * PART, (part + 1) * PART)
        def _(g):
            for r in range(CAP):
                s = picked_s[g, r]
                out[g, r] = keys[s]
                out[g, CAP + r] = values[s]

        leaving.append(
            pltpu.make_async_copy(out.at[groups], out_h.at[groups], out_sems.at[part])
        )
        leaving[-1].start()
    for copy in leaving:
        copy.wait()


def pack(me, prefix_blocks, block_owner, block_slot, pool_keys, pool_values):
    table = (block_owner.shape[0] // 128, 128)
    return pl.pallas_call(
        pack_kernel,
        out_shape=jax.ShapeDtypeStruct((POOL, LOAD, BLK, HD), bf16),
        in_specs=[SMEM] + [HBM] * 5,
        out_specs=HBM,
        scratch_shapes=[
            pltpu.VMEM(prefix_blocks.shape, i32),
            pltpu.VMEM(table, i32),
            pltpu.VMEM(table, i32),
            pltpu.VMEM(pool_keys.shape, bf16),
            pltpu.VMEM(pool_values.shape, bf16),
            pltpu.VMEM((POOL, PBLK), f32),
            pltpu.VMEM((POOL, 128), i32),
            pltpu.SMEM((POOL, 128), i32),
            pltpu.VMEM((POOL, LOAD, BLK, HD), bf16),
            pltpu.SemaphoreType.DMA((6,)),
            pltpu.SemaphoreType.DMA((POOL // PART,)),
        ],
        compiler_params=pltpu.CompilerParams(vmem_limit_bytes=WIDE),
        cost_estimate=cost(10**9, 5 * 10**6),
        name="pack_blocks",
    )(
        me.reshape(1),
        prefix_blocks,
        block_owner.reshape(table),
        block_slot.reshape(table),
        pool_keys,
        pool_values,
    )


def gather_kernel(info, evict, *refs):
    pieces = refs[:TENSOR]
    heads, start, sends, own_keys, own_values = refs[TENSOR:]
    t, count, me = info[0], info[1], info[2]
    lane = me & (LANES - 1)
    rows = TOK // TENSOR
    for k in range(TENSOR):
        begin = pl.multiple_of((t ^ k) * rows, rows)
        at = pl.ds(begin, rows)
        for h in range(GROUP):
            heads[pl.ds(pl.multiple_of(h * TOK + begin, rows), rows), :HD] = pieces[k][
                :, h * HD : (h + 1) * HD
            ]
        own_keys[at, :] = pieces[k][:, GROUP * HD : (GROUP + 1) * HD]
        own_values[at, :] = pieces[k][:, (GROUP + 1) * HD :]
    place = lax.broadcasted_iota(i32, (BLK, HD), 0)
    for j in range(NEWB):
        owner = evict[me, j] >> 8
        live = j * BLK + place < count
        for part, own in enumerate((own_keys, own_values)):
            block = own[j * BLK : (j + 1) * BLK, :]
            sends[(owner & (LANES - 1)) ^ lane, owner // LANES, part] = jnp.where(live, block.astype(f32), 0.0).astype(bf16)
    both = with_ones(own_values[...])
    row = lax.broadcasted_iota(i32, (TOK, TOK), 0)
    column = lax.broadcasted_iota(i32, (TOK, TOK), 1)

    @pl.loop(0, GROUP)
    def _(h):
        at = pl.ds(pl.multiple_of(h * TOK, TOK), TOK)
        scores = lax.dot_general(heads[at, :HD], own_keys[...], NT, preferred_element_type=f32)
        scores = jnp.where(column <= row, scores * SCALE, neg_big)
        top = jnp.max(scores, axis=1, keepdims=True).astype(bf16)
        heads[at, HD:] = jnp.broadcast_to(top, (TOK, HD))
        weights = jnp.exp2(scores - top.astype(f32)).astype(bf16)
        start[at, :] = jnp.dot(weights, both, preferred_element_type=f32)


def gather(info, evict_slots, pieces):
    return pl.pallas_call(
        gather_kernel,
        out_shape=[
            jax.ShapeDtypeStruct((GROUP * TOK, 2 * HD), bf16),
            jax.ShapeDtypeStruct((GROUP * TOK, 2 * HD), f32),
            jax.ShapeDtypeStruct((LANES, LEVELS, 2, BLK, HD), bf16),
        ],
        in_specs=[SMEM, SMEM] + [VMEM] * TENSOR,
        out_specs=[VMEM] * 3,
        scratch_shapes=[pltpu.VMEM((TOK, HD), bf16), pltpu.VMEM((TOK, HD), bf16)],
        compiler_params=pltpu.CompilerParams(vmem_limit_bytes=16 * 1024 * 1024),
        cost_estimate=cost(10**9, 4 * 10**6),
        name="gather_rows",
    )(info, evict_slots, *pieces)


def write_kernel(info, target, keys, values, arrived, out_keys, out_values):
    lane = info[2] & (LANES - 1)
    out_keys[...] = keys[...]
    out_values[...] = values[...]
    for level in range(LEVELS):
        for m in range(LANES):
            slot = target[level * LANES + (lane ^ m)]

            @pl.when(slot >= 0)
            def _():
                out_keys[slot] = arrived[level, m, 0]
                out_values[slot] = arrived[level, m, 1]


def write(info, target, pool_keys, pool_values, arrived):
    return pl.pallas_call(
        write_kernel,
        out_shape=[jax.ShapeDtypeStruct(pool_keys.shape, bf16)] * 2,
        in_specs=[SMEM, SMEM] + [VMEM] * 3,
        out_specs=[VMEM] * 2,
        compiler_params=pltpu.CompilerParams(vmem_limit_bytes=16 * 1024 * 1024),
        cost_estimate=cost(10**6, 4 * 10**6),
        name="write_blocks",
    )(info, target, pool_keys, pool_values, arrived)


KEYS = PBLK * BLK
ROWS = 1024
TILE = 256
SMALL = 256
SPLIT = 8


def attend_kernel(info, where_from, heads_h, start_h, got_h, out_h, *scratch):
    got, keys, values, heads, start, out, sems, got_sems, out_sems = scratch
    blocks = GROUP * TOK // ROWS
    part = got.shape[0] // SPLIT
    coming = []
    for i in range(SPLIT):
        at = pl.ds(i * part, part)
        coming.append(pltpu.make_async_copy(got_h.at[at], got.at[at], got_sems.at[i]))
    head_copies, start_copies = [], []
    for i in range(blocks):
        rows = pl.ds(i * ROWS, ROWS)
        head_copies.append(
            pltpu.make_async_copy(heads_h.at[rows], heads.at[rows], sems.at[i, 0])
        )
        start_copies.append(
            pltpu.make_async_copy(start_h.at[rows], start.at[rows], sems.at[i, 1])
        )
    for copy in coming + head_copies[:1]:
        copy.start()
    for copy in coming:
        copy.wait()
    for copy in head_copies[1:] + start_copies:
        copy.start()
    for b in range(PBLK):
        index = where_from[b]
        keys[b * BLK : (b + 1) * BLK, :] = got[index]
        values[b * BLK : (b + 1) * BLK, :] = got[index + CAP]
    live = lax.broadcasted_iota(i32, (TOK, HD), 0) < info[1]
    leaving = [
        pltpu.make_async_copy(
            out.at[:, pl.ds(h * HD, HD)], out_h.at[:, pl.ds(h * HD, HD)], out_sems.at[h]
        )
        for h in range(GROUP)
    ]

    def finish(h, summed):
        result = summed[:, :HD] / summed[:, HD:]
        out[:, h * HD : (h + 1) * HD] = jnp.where(live, result, 0.0).astype(bf16)

    for i in range(blocks):
        head_copies[i].wait()
        query = heads[i * ROWS : (i + 1) * ROWS, :HD]
        top = heads[i * ROWS : (i + 1) * ROWS, HD:].astype(f32)
        summed = None
        for j in range(KEYS // TILE):
            tile = slice(j * TILE, (j + 1) * TILE)
            part = lax.dot_general(query, keys[tile, :], NT, preferred_element_type=f32)
            weights = jnp.concatenate(
                [
                    jnp.exp2(part[:, c * HD : (c + 1) * HD] * SCALE - top)
                    for c in range(TILE // HD)
                ],
                axis=1,
            ).astype(bf16)
            more = jnp.dot(weights, with_ones(values[tile, :]), preferred_element_type=f32)
            summed = more if summed is None else summed + more
        start_copies[i].wait()
        summed = summed + start[i * ROWS : (i + 1) * ROWS, :]
        for h in range(ROWS // TOK):
            finish(i * (ROWS // TOK) + h, summed[h * TOK : (h + 1) * TOK, :])
        largest = jnp.max(summed[:, HD:])

        @pl.when(jnp.logical_not(largest < 1e30))
        def _():
            for h in range(ROWS // TOK):
                at = slice(i * ROWS + h * TOK, i * ROWS + (h + 1) * TOK)

                def one(j, state):
                    best, summed = state
                    tile = pl.ds(pl.multiple_of(j * SMALL, SMALL), SMALL)
                    part = (
                        lax.dot_general(
                            heads[at, :HD], keys[tile, :], NT, preferred_element_type=f32
                        )
                        * SCALE
                    )
                    above = jnp.maximum(best, jnp.max(part, axis=1, keepdims=True))
                    weights = jnp.exp2(part - above).astype(bf16)
                    summed = summed * jnp.exp2(best - above) + jnp.dot(
                        weights, with_ones(values[tile, :]), preferred_element_type=f32
                    )
                    return above, summed

                best, summed = lax.fori_loop(
                    0,
                    KEYS // SMALL,
                    one,
                    (heads[at, HD : HD + 1].astype(f32), start[at, :]),
                )
                finish(i * (ROWS // TOK) + h, summed)

        for h in range(i * (ROWS // TOK), (i + 1) * (ROWS // TOK)):
            leaving[h].start()
    for copy in leaving:
        copy.wait()


def attend(info, where_from, heads, start, got):
    blocks = got.shape[0] * got.shape[1]
    return pl.pallas_call(
        attend_kernel,
        out_shape=jax.ShapeDtypeStruct((TOK, GROUP * HD), bf16),
        in_specs=[SMEM, SMEM, HBM, HBM, HBM],
        out_specs=HBM,
        scratch_shapes=[
            pltpu.VMEM((blocks, BLK, HD), bf16),
            pltpu.VMEM((KEYS, HD), bf16),
            pltpu.VMEM((KEYS, HD), bf16),
            pltpu.VMEM(heads.shape, bf16),
            pltpu.VMEM(start.shape, f32),
            pltpu.VMEM((TOK, GROUP * HD), bf16),
            pltpu.SemaphoreType.DMA((GROUP * TOK // ROWS, 2)),
            pltpu.SemaphoreType.DMA((SPLIT,)),
            pltpu.SemaphoreType.DMA((GROUP,)),
        ],
        compiler_params=pltpu.CompilerParams(vmem_limit_bytes=WIDE),
        cost_estimate=cost(9 * 10**9, 6 * 10**6, 9 * 10**6),
        name="attend",
    )(info, where_from, heads, start, got.reshape(blocks, BLK, HD))


def local(
    queries,
    new_keys,
    new_values,
    pool_keys,
    pool_values,
    prefix_blocks,
    block_owner,
    block_slot,
    evict_slots,
    tok_counts,
):
    me = lax.axis_index("pool").astype(i32)
    t = lax.axis_index("tensor").astype(i32)
    share = TOK // TENSOR
    info = jnp.stack([t, tok_counts[me], me])

    send = pack(me, prefix_blocks, block_owner, block_slot, pool_keys, pool_values)
    send, queries, new_keys, new_values = lax.optimization_barrier(
        (send, queries, new_keys, new_values)
    )
    got = lax.all_to_all(send, "pool", split_axis=0, concat_axis=0, tiled=True)

    pieces = []
    for k in range(TENSOR):
        head = t ^ k
        piece = jnp.concatenate(
            [
                lax.dynamic_slice_in_dim(queries, head * GROUP * HD, GROUP * HD, 1),
                lax.dynamic_slice_in_dim(new_keys, head * HD, HD, 1),
                lax.dynamic_slice_in_dim(new_values, head * HD, HD, 1),
            ],
            axis=1,
        )
        if k:
            piece = lax.ppermute(piece, "tensor", [(s, s ^ k) for s in range(TENSOR)])
        pieces.append(piece)

    sources = jnp.arange(POOL, dtype=i32)
    my_owners = block_owner[prefix_blocks[me]]
    ends = jnp.sum((my_owners[None, :] <= sources[:, None]).astype(i32), axis=1)
    starts = jnp.sum((my_owners[None, :] < sources[:, None]).astype(i32), axis=1)
    nth = jnp.arange(PBLK, dtype=i32)
    which = jnp.sum((ends[None, :] <= nth[:, None]).astype(i32), axis=1)
    base = jnp.max(jnp.where(starts[None, :] <= nth[:, None], starts[None, :], 0), axis=1)
    where_from = which * LOAD + nth - base

    target = jnp.max(jnp.where(evict_slots // SLOTS == me, evict_slots % SLOTS, -1), axis=1)

    heads, start, sends = gather(info, evict_slots, pieces)
    turned = [sends[0]] + [
        lax.ppermute(sends[m], "pool", [(s, s ^ m) for s in range(POOL)])
        for m in range(1, LANES)
    ]
    sends = jnp.stack(turned, axis=1)
    got, sends = lax.optimization_barrier((got, sends))
    columns = [[level * LANES + lane for level in range(LEVELS)] for lane in range(LANES)]
    arrived = lax.all_to_all(
        sends, "pool", split_axis=0, concat_axis=0, tiled=True, axis_index_groups=columns
    )
    result = attend(info, where_from, heads, start, got)
    result, arrived = lax.optimization_barrier((result, arrived))
    result = result.reshape(TENSOR, share, GROUP * HD)
    attended = lax.all_to_all(result, "tensor", split_axis=0, concat_axis=0, tiled=True)
    attended = jnp.transpose(attended, (1, 0, 2)).reshape(share, H * HD)
    new_pool_keys, new_pool_values = write(info, target, pool_keys, pool_values, arrived)
    return (attended, new_pool_keys, new_pool_values)


def solution(mesh):
    placed = (
        P(("pool", "tensor"), None),
        P(("pool", "tensor"), None),
        P(("pool", "tensor"), None),
        P("pool", None, "tensor"),
        P("pool", None, "tensor"),
        P(),
        P(),
        P(),
        P(),
        P(),
    )
    return jax.shard_map(
        local,
        mesh=mesh,
        in_specs=placed,
        out_specs=(
            P(("pool", "tensor"), None),
            P("pool", None, "tensor"),
            P("pool", None, "tensor"),
        ),
        check_vma=False,
    )
```

```python
import functools

import jax
import jax.numpy as jnp
from jax import lax
from jax.experimental import pallas as pl
from jax.experimental.pallas import tpu as pltpu
from jax.sharding import PartitionSpec as P

H = 64
KVH = 8
HD = 128
GROUP = H // KVH
BLK = 16
POOL = 32
LANES = 4
LEVELS = POOL // LANES
TENSOR = 8
SLOTS = 256
PBLK = 256
CAP = 12
TOK = 256
NEWB = TOK // BLK
LOAD = 2 * CAP
PART = 4
WIDE = 57 * 1024 * 1024
SCALE = HD ** (-0.5) * 1.4426950408889634
neg_big = -1e30

bf16 = jnp.bfloat16
f32 = jnp.float32
i32 = jnp.int32

VMEM = pl.BlockSpec(memory_space=pltpu.VMEM)
SMEM = pl.BlockSpec(memory_space=pltpu.SMEM)
HBM = pl.BlockSpec(memory_space=pltpu.HBM)
NT = (((1,), (1,)), ((), ()))


def with_ones(values):
    return jnp.concatenate([values, jnp.ones(values.shape, bf16)], axis=1)


def cost(flops, moved, exps=0):
    return pl.CostEstimate(flops=flops, bytes_accessed=moved, transcendentals=exps)


def pack_kernel(me, prefix_h, owner_h, slot_h, keys_h, values_h, out_h, *scratch):
    prefix, owner, slot, keys, values, wanted, picked, picked_s, out, sems, out_sems = scratch
    sources = (prefix_h, owner_h, slot_h, keys_h, values_h)
    copies = [
        pltpu.make_async_copy(source, target, sems.at[i])
        for i, (source, target) in enumerate(zip(sources, scratch[:5]))
    ]
    for copy in copies:
        copy.start()
    for copy in copies[:3]:
        copy.wait()
    rows, lanes = owner.shape
    mine = jnp.where(owner[...] == me[0], slot[...] + 1, 0).astype(f32).astype(bf16)
    lane_of = lax.broadcasted_iota(i32, (lanes, PBLK), 0)
    row_of = lax.broadcasted_iota(i32, (rows, PBLK), 0)
    for g in range(POOL):
        index = prefix[g : g + 1, :]
        low = index & (lanes - 1)
        high = index >> 7
        hot = jnp.where(lane_of == low, 1.0, 0.0).astype(bf16)
        found = jnp.dot(mine, hot, preferred_element_type=f32)
        wanted[g : g + 1, :] = jnp.sum(
            jnp.where(row_of == high, found, 0.0), axis=0, keepdims=True
        )
    place = wanted[...]
    held = place > 0.5
    before = lax.broadcasted_iota(i32, (PBLK, PBLK), 0)
    after = lax.broadcasted_iota(i32, (PBLK, PBLK), 1)
    triangle = jnp.where(before <= after, 1.0, 0.0).astype(bf16)
    rank = jnp.dot(
        jnp.where(held, 1.0, 0.0).astype(bf16), triangle, preferred_element_type=f32
    )
    rank = jnp.where(held, rank, 0.0)
    lane = lax.broadcasted_iota(i32, (POOL, 128), 1)
    chosen = jnp.zeros((POOL, 128), f32)
    for r in range(CAP):
        one = jnp.sum(jnp.where(rank == r + 1.0, place - 1.0, 0.0), axis=1, keepdims=True)
        chosen = jnp.where(lane == r, one, chosen)
    picked[...] = chosen.astype(i32)
    listed = pltpu.make_async_copy(picked, picked_s, sems.at[5])
    listed.start()
    listed.wait()
    for copy in copies[3:]:
        copy.wait()

    leaving = []
    for part in range(POOL // PART):
        groups = pl.ds(part * PART, PART)

        @pl.loop(part * PART, (part + 1) * PART)
        def _(g):
            for r in range(CAP):
                s = picked_s[g, r]
                out[g, r] = keys[s]
                out[g, CAP + r] = values[s]

        leaving.append(
            pltpu.make_async_copy(out.at[groups], out_h.at[groups], out_sems.at[part])
        )
        leaving[-1].start()
    for copy in leaving:
        copy.wait()


def pack(me, prefix_blocks, block_owner, block_slot, pool_keys, pool_values):
    table = (block_owner.shape[0] // 128, 128)
    return pl.pallas_call(
        pack_kernel,
        out_shape=jax.ShapeDtypeStruct((POOL, LOAD, BLK, HD), bf16),
        in_specs=[SMEM] + [HBM] * 5,
        out_specs=HBM,
        scratch_shapes=[
            pltpu.VMEM(prefix_blocks.shape, i32),
            pltpu.VMEM(table, i32),
            pltpu.VMEM(table, i32),
            pltpu.VMEM(pool_keys.shape, bf16),
            pltpu.VMEM(pool_values.shape, bf16),
            pltpu.VMEM((POOL, PBLK), f32),
            pltpu.VMEM((POOL, 128), i32),
            pltpu.SMEM((POOL, 128), i32),
            pltpu.VMEM((POOL, LOAD, BLK, HD), bf16),
            pltpu.SemaphoreType.DMA((6,)),
            pltpu.SemaphoreType.DMA((POOL // PART,)),
        ],
        compiler_params=pltpu.CompilerParams(vmem_limit_bytes=WIDE),
        cost_estimate=cost(10**9, 5 * 10**6),
        name="pack_blocks",
    )(
        me.reshape(1),
        prefix_blocks,
        block_owner.reshape(table),
        block_slot.reshape(table),
        pool_keys,
        pool_values,
    )


def gather_kernel(info, evict, *refs):
    pieces = refs[:TENSOR]
    heads, own_keys, own_values, sends = refs[TENSOR:]
    t, count, me = info[0], info[1], info[2]
    lane = me & (LANES - 1)
    rows = TOK // TENSOR
    for k in range(TENSOR):
        begin = pl.multiple_of((t ^ k) * rows, rows)
        at = pl.ds(begin, rows)
        for h in range(GROUP):
            heads[pl.ds(pl.multiple_of(h * TOK + begin, rows), rows), :] = pieces[k][
                :, h * HD : (h + 1) * HD
            ]
        own_keys[at, :] = pieces[k][:, GROUP * HD : (GROUP + 1) * HD]
        own_values[at, :] = pieces[k][:, (GROUP + 1) * HD :]
    place = lax.broadcasted_iota(i32, (BLK, HD), 0)
    for j in range(NEWB):
        owner = evict[me, j] >> 8
        live = j * BLK + place < count
        for part, own in enumerate((own_keys, own_values)):
            block = own[j * BLK : (j + 1) * BLK, :]
            sends[(owner & (LANES - 1)) ^ lane, owner // LANES, part] = jnp.where(live, block.astype(f32), 0.0).astype(bf16)


def gather(info, evict_slots, pieces):
    return pl.pallas_call(
        gather_kernel,
        out_shape=[
            jax.ShapeDtypeStruct((GROUP * TOK, HD), bf16),
            jax.ShapeDtypeStruct((TOK, HD), bf16),
            jax.ShapeDtypeStruct((TOK, HD), bf16),
            jax.ShapeDtypeStruct((LANES, LEVELS, 2, BLK, HD), bf16),
        ],
        in_specs=[SMEM, SMEM] + [VMEM] * TENSOR,
        out_specs=[VMEM] * 4,
        compiler_params=pltpu.CompilerParams(vmem_limit_bytes=16 * 1024 * 1024),
        cost_estimate=cost(10**9, 4 * 10**6),
        name="gather_rows",
    )(info, evict_slots, *pieces)


def write_kernel(info, target, keys, values, arrived, out_keys, out_values):
    lane = info[2] & (LANES - 1)
    out_keys[...] = keys[...]
    out_values[...] = values[...]
    for level in range(LEVELS):
        for m in range(LANES):
            slot = target[level * LANES + (lane ^ m)]

            @pl.when(slot >= 0)
            def _():
                out_keys[slot] = arrived[level, m, 0]
                out_values[slot] = arrived[level, m, 1]


def write(info, target, pool_keys, pool_values, arrived):
    return pl.pallas_call(
        write_kernel,
        out_shape=[jax.ShapeDtypeStruct(pool_keys.shape, bf16)] * 2,
        in_specs=[SMEM, SMEM] + [VMEM] * 3,
        out_specs=[VMEM] * 2,
        compiler_params=pltpu.CompilerParams(vmem_limit_bytes=16 * 1024 * 1024),
        cost_estimate=cost(10**6, 4 * 10**6),
        name="write_blocks",
    )(info, target, pool_keys, pool_values, arrived)


KEYS = PBLK * BLK
ROWS = 1024
TILE = 256
SPLIT = 8


def attend_kernel(info, where_from, heads_h, own_keys_h, own_values_h, got_h, out_h, *scratch):
    got, keys, values, heads, own_keys, own_values, shift, start, out, sems, got_sems, out_sem = (
        scratch
    )
    blocks = GROUP * TOK // ROWS
    part = got.shape[0] // SPLIT
    coming = []
    for i in range(SPLIT):
        at = pl.ds(i * part, part)
        coming.append(pltpu.make_async_copy(got_h.at[at], got.at[at], got_sems.at[i]))
    first = [
        pltpu.make_async_copy(source, target, sems.at[i])
        for i, (source, target) in enumerate(
            ((own_keys_h, own_keys), (own_values_h, own_values), (heads_h, heads))
        )
    ]
    for copy in first + coming:
        copy.start()
    for copy in first:
        copy.wait()

    both = with_ones(own_values[...])
    row = lax.broadcasted_iota(i32, (TOK, TOK), 0)
    column = lax.broadcasted_iota(i32, (TOK, TOK), 1)
    for h in range(GROUP):
        at = slice(h * TOK, (h + 1) * TOK)
        scores = lax.dot_general(heads[at, :], own_keys[...], NT, preferred_element_type=f32)
        scores = jnp.where(column <= row, scores * SCALE, neg_big)
        top = jnp.max(scores, axis=1, keepdims=True)
        shift[at, :] = jnp.broadcast_to(top, (TOK, HD))
        weights = jnp.exp2(scores - top).astype(bf16)
        start[at, :] = jnp.dot(weights, both, preferred_element_type=f32)

    for copy in coming:
        copy.wait()
    for b in range(PBLK):
        index = where_from[b]
        keys[b * BLK : (b + 1) * BLK, :] = got[index]
        values[b * BLK : (b + 1) * BLK, :] = got[index + CAP]
    live = lax.broadcasted_iota(i32, (TOK, HD), 0) < info[1]
    largest = []
    def result_of(summed):
        return jnp.where(live, summed[:, :HD] / summed[:, HD:], 0.0).astype(bf16)

    for i in range(blocks):
        query = heads[i * ROWS : (i + 1) * ROWS, :]
        top = shift[i * ROWS : (i + 1) * ROWS, :]
        summed = start[i * ROWS : (i + 1) * ROWS, :]
        for j in range(KEYS // TILE):
            tile = slice(j * TILE, (j + 1) * TILE)
            part = lax.dot_general(query, keys[tile, :], NT, preferred_element_type=f32)
            weights = jnp.concatenate(
                [
                    jnp.exp2(part[:, c * HD : (c + 1) * HD] * SCALE - top)
                    for c in range(TILE // HD)
                ],
                axis=1,
            ).astype(bf16)
            summed = summed + jnp.dot(
                weights, with_ones(values[tile, :]), preferred_element_type=f32
            )
        for h in range(ROWS // TOK):
            head = i * (ROWS // TOK) + h
            out[:, head * HD : (head + 1) * HD] = result_of(summed[h * TOK : (h + 1) * TOK, :])
        largest.append(jnp.max(summed[:, HD:]))

    @pl.when(jnp.logical_not(functools.reduce(jnp.maximum, largest) < 1e30))
    def _():
        @pl.loop(0, GROUP)
        def _(h):
            at = pl.ds(pl.multiple_of(h * TOK, TOK), TOK)

            def one(j, state):
                best, summed = state
                tile = pl.ds(pl.multiple_of(j * TILE, TILE), TILE)
                part = (
                    lax.dot_general(heads[at, :], keys[tile, :], NT, preferred_element_type=f32)
                    * SCALE
                )
                above = jnp.maximum(best, jnp.max(part, axis=1, keepdims=True))
                weights = jnp.exp2(part - above).astype(bf16)
                summed = summed * jnp.exp2(best - above) + jnp.dot(
                    weights, with_ones(values[tile, :]), preferred_element_type=f32
                )
                return above, summed

            best, summed = lax.fori_loop(0, KEYS // TILE, one, (shift[at, :1], start[at, :]))
            out[:, pl.ds(pl.multiple_of(h * HD, HD), HD)] = result_of(summed)

    leaving = pltpu.make_async_copy(out, out_h, out_sem)
    leaving.start()
    leaving.wait()


def attend(info, where_from, heads, own_keys, own_values, got):
    blocks = got.shape[0] * got.shape[1]
    return pl.pallas_call(
        attend_kernel,
        out_shape=jax.ShapeDtypeStruct((TOK, GROUP * HD), bf16),
        in_specs=[SMEM, SMEM] + [HBM] * 4,
        out_specs=HBM,
        scratch_shapes=[
            pltpu.VMEM((blocks, BLK, HD), bf16),
            pltpu.VMEM((KEYS, HD), bf16),
            pltpu.VMEM((KEYS, HD), bf16),
            pltpu.VMEM(heads.shape, bf16),
            pltpu.VMEM((TOK, HD), bf16),
            pltpu.VMEM((TOK, HD), bf16),
            pltpu.VMEM(heads.shape, f32),
            pltpu.VMEM((GROUP * TOK, 2 * HD), f32),
            pltpu.VMEM((TOK, GROUP * HD), bf16),
            pltpu.SemaphoreType.DMA((3,)),
            pltpu.SemaphoreType.DMA((SPLIT,)),
            pltpu.SemaphoreType.DMA,
        ],
        compiler_params=pltpu.CompilerParams(vmem_limit_bytes=WIDE),
        cost_estimate=cost(9 * 10**9, 6 * 10**6, 9 * 10**6),
        name="attend",
    )(info, where_from, heads, own_keys, own_values, got.reshape(blocks, BLK, HD))


def local(
    queries,
    new_keys,
    new_values,
    pool_keys,
    pool_values,
    prefix_blocks,
    block_owner,
    block_slot,
    evict_slots,
    tok_counts,
):
    me = lax.axis_index("pool").astype(i32)
    t = lax.axis_index("tensor").astype(i32)
    share = TOK // TENSOR
    info = jnp.stack([t, tok_counts[me], me])

    send = pack(me, prefix_blocks, block_owner, block_slot, pool_keys, pool_values)
    send, queries, new_keys, new_values = lax.optimization_barrier(
        (send, queries, new_keys, new_values)
    )
    got = lax.all_to_all(send, "pool", split_axis=0, concat_axis=0, tiled=True)

    pieces = []
    for k in range(TENSOR):
        head = t ^ k
        piece = jnp.concatenate(
            [
                lax.dynamic_slice_in_dim(queries, head * GROUP * HD, GROUP * HD, 1),
                lax.dynamic_slice_in_dim(new_keys, head * HD, HD, 1),
                lax.dynamic_slice_in_dim(new_values, head * HD, HD, 1),
            ],
            axis=1,
        )
        if k:
            piece = lax.ppermute(piece, "tensor", [(s, s ^ k) for s in range(TENSOR)])
        pieces.append(piece)

    sources = jnp.arange(POOL, dtype=i32)
    my_owners = block_owner[prefix_blocks[me]]
    ends = jnp.sum((my_owners[None, :] <= sources[:, None]).astype(i32), axis=1)
    starts = jnp.sum((my_owners[None, :] < sources[:, None]).astype(i32), axis=1)
    nth = jnp.arange(PBLK, dtype=i32)
    which = jnp.sum((ends[None, :] <= nth[:, None]).astype(i32), axis=1)
    base = jnp.max(jnp.where(starts[None, :] <= nth[:, None], starts[None, :], 0), axis=1)
    where_from = which * LOAD + nth - base

    target = jnp.max(jnp.where(evict_slots // SLOTS == me, evict_slots % SLOTS, -1), axis=1)

    heads, own_keys, own_values, sends = gather(info, evict_slots, pieces)
    turned = [sends[0]] + [
        lax.ppermute(sends[m], "pool", [(s, s ^ m) for s in range(POOL)])
        for m in range(1, LANES)
    ]
    sends = jnp.stack(turned, axis=1)
    got, sends = lax.optimization_barrier((got, sends))
    columns = [[level * LANES + lane for level in range(LEVELS)] for lane in range(LANES)]
    arrived = lax.all_to_all(
        sends, "pool", split_axis=0, concat_axis=0, tiled=True, axis_index_groups=columns
    )
    result = attend(info, where_from, heads, own_keys, own_values, got)
    result, arrived = lax.optimization_barrier((result, arrived))
    result = result.reshape(TENSOR, share, GROUP * HD)
    attended = lax.all_to_all(result, "tensor", split_axis=0, concat_axis=0, tiled=True)
    attended = jnp.transpose(attended, (1, 0, 2)).reshape(share, H * HD)
    new_pool_keys, new_pool_values = write(info, target, pool_keys, pool_values, arrived)
    return (attended, new_pool_keys, new_pool_values)


def solution(mesh):
    placed = (
        P(("pool", "tensor"), None),
        P(("pool", "tensor"), None),
        P(("pool", "tensor"), None),
        P("pool", None, "tensor"),
        P("pool", None, "tensor"),
        P(),
        P(),
        P(),
        P(),
        P(),
    )
    return jax.shard_map(
        local,
        mesh=mesh,
        in_specs=placed,
        out_specs=(
            P(("pool", "tensor"), None),
            P("pool", None, "tensor"),
            P("pool", None, "tensor"),
        ),
        check_vma=False,
    )
```
